256 devices in a mesh: pts: 64 (over z, y_lo, x), days: 4 (over y_hi, core).
Axes of the slice: x: 4, y: 4 (y_hi: 2, y_lo: 2; y = y_hi * 2 + y_lo), z: 8, core: 2. Of those that a mesh axis runs over, the one named last changes fastest.
Arguments:
- series: bfloat16 [131072, 4096], P('pts', 'days')
- partner: int32 [64], replicated, may hold values from 0 to 63, as said below
Outputs:
- correlation: float32 [131072, 2048], P(('pts', 'days'))
- degree: float32 [131072], P(('pts', 'days'))
The draws below stay inside these ranges and needn't reach their ends.
Inputs may be any that keep to these rules, and one draw needn't show every extreme that they name: partner pairs the 64 blocks: partner[partner[b]] = b and partner[b] != b for every block b.
All inputs are finite; a program needn't handle non-finite values.
Results may differ from the reference program's by a relative error of at most 0.00041.
Values may be sent and summed in bfloat16 or wider, within the bound.
A program may use at most 128 MiB of HBM per device.

```python
import jax
import jax.numpy as jnp
from jax import lax

BP = 2048
DAYS = 4096
POINTS = 131072
N_PTS = 64


def draw_series(key, part):
    key = jax.random.fold_in(key, 11)
    keys = jax.random.split(key, 5)
    loading = jax.random.uniform(keys[0], (POINTS, 1), jnp.float32, -1.0, 1.0)
    offset = jax.random.uniform(keys[1], (POINTS, 1), jnp.float32, -20.0, 20.0)
    scale = jnp.exp(jax.random.uniform(keys[2], (POINTS, 1), jnp.float32, 0.0, jnp.log(10.0)))
    noise = jnp.clip(jax.random.normal(keys[3], (POINTS, DAYS), jnp.float32), -6.0, 6.0)
    common = jnp.clip(jax.random.normal(keys[4], (1, DAYS), jnp.float32), -6.0, 6.0)
    ramp = 1.0 + 2.0 * jnp.arange(DAYS, dtype=jnp.float32) / (DAYS - 1)
    values = offset + scale * ramp[None, :] * (noise + loading * common)
    return values.astype(jnp.bfloat16)


def draw_partner(key, part):
    key = jax.random.fold_in(key, 23)
    first_key, second_key = jax.random.split(key)
    last = N_PTS - 1
    round_index = jax.random.randint(first_key, (), 0, last, dtype=jnp.int32)
    labels = jnp.arange(N_PTS, dtype=jnp.int32)
    circle = jnp.where(labels == last, round_index, jnp.where(labels == round_index, last, (2 * round_index - labels) % last))
    relabel = jax.random.permutation(second_key, N_PTS).astype(jnp.int32)
    result = jnp.zeros((N_PTS,), jnp.int32).at[relabel].set(relabel[circle])
    return result.astype(jnp.int32)


def setup_inputs(seed: int = 0) -> dict:
    splits = jax.random.split(jax.random.key(seed), 3)
    return {
        "series": draw_series(jax.random.fold_in(splits[2], 71), 0),
        "partner": draw_partner(jax.random.fold_in(splits[2], 71), 0),
    }


def reference(series, partner):
    values = series.astype(jnp.float32)
    average = lax.optimization_barrier(jnp.mean(values, axis=1, keepdims=True))
    centred = values - average
    variance = lax.optimization_barrier(jnp.mean(centred * centred, axis=1, keepdims=True))
    normed = (centred * lax.rsqrt(variance + 1e-06)).astype(jnp.bfloat16)
    blocks = normed.reshape(N_PTS, BP, DAYS)

    def one_block(item):
        own_block, other_index = item
        other_block = jnp.take(blocks, other_index, axis=0)
        result = jnp.dot(own_block.astype(jnp.float32), other_block.astype(jnp.float32).T, precision=lax.Precision.HIGHEST)
        return result / DAYS
    correlation = lax.map(one_block, (blocks, partner)).reshape(POINTS, BP)
    degree = lax.optimization_barrier(jnp.sum(correlation * correlation, axis=1))
    return (correlation, degree)
```

```python
import functools

import jax
import jax.numpy as jnp
from jax import lax
from jax.experimental import pallas as pl
from jax.experimental.pallas import tpu as pltpu
from jax.sharding import Mesh, PartitionSpec as P

epsilon = 1e-06

PTS = ("z", "yl", "x")
DAYS = ("yh", "core")
FIRST_PARTS = 2
CHUNKS = 4
MESH = pl.DeviceIdType.MESH


def remote(src, dst, send, recv, **device):
    return pltpu.make_async_remote_copy(
        src_ref=src, dst_ref=dst, send_sem=send, recv_sem=recv, device_id=device, device_id_type=MESH
    )


def wait_bytes(ref, sem):
    pltpu.make_async_copy(ref, ref, sem).wait()


def kernel(
    sizes,
    partner,
    series,
    out,
    stats,
    final,
    normed,
    inboxes,
    chosen,
    landed,
    own,
    full,
    stat_send,
    stat_recv,
    own_send,
    own_recv,
    first_send,
    first_recv,
    second_send,
    second_recv,
    y_send,
    y_recv,
    core_send,
    core_recv,
):
    Z, YL, X, YH, C = sizes
    z, yl, x, yh, core = (lax.axis_index(name) for name in PTS + DAYS)
    groups = Z * YL * X
    flat = Z * X
    quarters = YH * C
    points, days = series.shape
    piece = points // groups
    rows = points // quarters
    width = days // FIRST_PARTS
    span = days // CHUNKS
    block = (z * YL + yl) * X + x
    zx = z * X + x
    day = yh * C + core
    here = yl * quarters + day

    def peer(o):
        return (
            lax.rem(z + lax.rem(o * 3, Z), Z),
            lax.rem(yl + lax.rem(o // Z, YL), YL),
            lax.rem(x + o // (Z * YL), X),
        )

    def other_day(o):
        to = lax.rem(day + o, quarters)
        return to, lax.div(to, C), lax.rem(to, C)

    barrier = pltpu.get_barrier_semaphore()

    def greet(o, carry):
        pz, py, px = peer(o)
        pl.semaphore_signal(barrier, inc=1, device_id={"z": pz, "yl": py, "x": px}, device_id_type=MESH)
        return carry

    lax.fori_loop(1, groups, greet, 0)
    for o in range(1, quarters):
        _, ph, pc = other_day(o)
        pl.semaphore_signal(barrier, inc=1, device_id={"yh": ph, "core": pc}, device_id_type=MESH)
    pl.semaphore_signal(barrier, inc=1, device_id={"yl": 1 - yl, "yh": 1 - yh}, device_id_type=MESH)

    tile = 128
    eye = lax.broadcasted_iota(jnp.int32, (tile, tile), 0) == lax.broadcasted_iota(jnp.int32, (tile, tile), 1)

    def to_lanes(column):
        return jnp.sum(jnp.where(eye, column, 0.0), axis=0, keepdims=True)

    def to_rows(line):
        return jnp.sum(jnp.where(eye, line, 0.0), axis=1, keepdims=True)

    def local_stats(g, carry):
        values = series[pl.ds(pl.multiple_of(g * tile, tile), tile), :].astype(jnp.float32)
        mean = jnp.sum(values, axis=1, keepdims=True) / days
        centred = values - mean
        squares = jnp.sum(centred * centred, axis=1, keepdims=True)
        stats[day, 0, pl.ds(g, 1), :] = to_lanes(mean)
        stats[day, 1, pl.ds(g, 1), :] = to_lanes(squares)
        return carry

    lax.fori_loop(0, points // tile, local_stats, 0)

    pl.semaphore_wait(barrier, groups - 1 + quarters - 1 + 1)

    for o in range(1, quarters):
        _, ph, pc = other_day(o)
        remote(stats.at[day], stats.at[day], stat_send, stat_recv.at[o - 1], yh=ph, core=pc).start()
    for o in range(1, quarters):
        wait_bytes(stats.at[0], stat_recv.at[o - 1])

    means = [stats[d, 0] for d in range(quarters)]
    average = sum(means) / quarters
    spread = sum(stats[d, 1] for d in range(quarters))
    spread += days * sum((m - average) * (m - average) for m in means)
    final[0] = average
    final[1] = lax.rsqrt(spread / (days * quarters) + epsilon)

    def normalise(g, carry):
        at = pl.ds(pl.multiple_of(g * tile, tile), tile)
        values = series[at, :].astype(jnp.float32)
        centred = values - to_rows(final[0, pl.ds(g, 1), :])
        normed[at, :] = (centred * to_rows(final[1, pl.ds(g, 1), :])).astype(jnp.bfloat16)
        return carry

    lax.fori_loop(0, points // tile, normalise, 0)

    def first_part(part):
        cols = pl.ds(part * width, width)

        def send(o, carry):
            pz, py, px = peer(o)
            to = py * flat + pz * X + px
            remote(
                normed.at[pl.ds(pl.multiple_of(to * piece, piece), piece), cols],
                inboxes[part].at[block],
                first_send,
                first_recv.at[part],
                z=pz,
                yl=py,
                x=px,
            ).start()
            return carry

        lax.fori_loop(1, groups, send, 0)

    first_part(0)
    for o in range(1, quarters):
        to, ph, pc = other_day(o)
        remote(
            normed.at[pl.ds(pl.multiple_of(to * rows, rows), rows), :],
            own.at[day],
            own_send,
            own_recv,
            yh=ph,
            core=pc,
        ).start()
    for part in range(1, FIRST_PARTS):
        first_part(part)
    mine = yl * flat + zx
    for part in range(FIRST_PARTS):
        cols = pl.ds(part * width, width)
        inboxes[part][block] = normed[pl.ds(pl.multiple_of(mine * piece, piece), piece), cols]
    own[day] = normed[pl.ds(pl.multiple_of(day * rows, rows), rows), :]

    def second_hop(k):
        inbox = inboxes[k * span // width]
        cols = pl.ds(k * span % width, span)

        def pick(t, carry):
            to_z, to_y, to_x = t // (YL * X), lax.rem(t // X, YL), lax.rem(t, X)
            chosen[k, to_z * X + to_x, to_y] = inbox[partner[t], :, cols]
            return carry

        lax.fori_loop(0, groups, pick, 0)
        for half in range(YL):
            landed[k, half, zx] = chosen[k, zx, half]

        def send(o, carry):
            pz = lax.rem(z + lax.rem(o * 3, Z), Z)
            px = lax.rem(x + o // Z, X)
            remote(
                chosen.at[k, pz * X + px],
                landed.at[k, :, zx],
                second_send,
                second_recv.at[k],
                z=pz,
                x=px,
            ).start()
            return carry

        lax.fori_loop(1, flat, send, 0)

    def y_source(j):
        if j == 0:
            return yl * quarters + (1 - yh) * C + core
        return (1 - yl) * quarters + (j - 1) * C + core

    def spread_y(k):
        wait_bytes(chosen.at[k, pl.ds(0, flat - 1)], second_recv.at[k])
        remote(
            landed.at[k, yl], full.at[k, here], y_send, y_recv.at[k, 0], yh=1 - yh
        ).start()
        for to in range(YH):
            remote(
                landed.at[k, 1 - yl], full.at[k, here], y_send, y_recv.at[k, 1 + yh], yl=1 - yl, yh=to
            ).start()
        remote(landed.at[k, yl], full.at[k, here], core_send, core_recv.at[k], core=1 - core).start()
        full[k, here] = landed[k, yl]

    def spread_core(k):
        for j in range(3):
            wait_bytes(full.at[k, 0], y_recv.at[k, j])
            at = y_source(j)
            remote(full.at[k, at], full.at[k, at], core_send, core_recv.at[k], core=1 - core).start()

    columns = min(256, flat * piece)
    tiles = flat * piece // columns

    def multiply(k):
        wait_bytes(full.at[k, pl.ds(0, 4)], core_recv.at[k])

        def one(n, carry):
            half, t = n // tiles, lax.rem(n, tiles)
            group = columns // piece
            total = None
            for q in range(quarters):
                right = full[k, half * quarters + q, pl.ds(t * group, group)].reshape(columns, span)
                term = lax.dot_general(
                    own[q, :, pl.ds(k * span, span)],
                    right,
                    (((1,), (1,)), ((), ())),
                    preferred_element_type=jnp.float32,
                )
                total = term if total is None else total + term
            at = pl.ds(pl.multiple_of(n * columns, columns), columns)
            out[:, at] = total if k == 0 else out[:, at] + total
            return carry

        lax.fori_loop(0, YL * tiles, one, 0)

    ahead = 1
    for step in range(CHUNKS + ahead + 2):
        if step < CHUNKS:
            if step * span % width == 0:
                part = step * span // width
                wait_bytes(inboxes[part].at[pl.ds(0, groups - 1)], first_recv.at[part])
            second_hop(step)
        k = step - ahead
        if 0 <= k < CHUNKS:
            spread_y(k)
        k = step - ahead - 1
        if 0 <= k < CHUNKS:
            spread_core(k)
        k = step - ahead - 2
        if 0 <= k < CHUNKS:
            if k == 0:
                wait_bytes(own.at[pl.ds(0, quarters - 1)], own_recv)
            multiply(k)

    wait_bytes(stats.at[pl.ds(0, quarters - 1)], stat_send)
    wait_bytes(own.at[pl.ds(0, quarters - 1)], own_send)
    wait_bytes(normed.at[pl.ds(0, (groups - 1) * piece)], first_send)
    wait_bytes(chosen.at[:, pl.ds(0, flat - 1)], second_send)
    wait_bytes(full.at[:, pl.ds(0, 3)], y_send)
    wait_bytes(full.at[:, pl.ds(0, 4)], core_send)


def on_device(sizes, series, partner):
    Z, YL, X, YH, C = sizes
    groups, flat, quarters = Z * YL * X, Z * X, YH * C
    points, days = series.shape
    piece, rows, span = points // groups, points // quarters, days // CHUNKS
    bf16 = jnp.bfloat16
    dma = pltpu.SemaphoreType.DMA
    total = pl.pallas_call(
        functools.partial(kernel, sizes),
        out_shape=jax.ShapeDtypeStruct((rows, points), jnp.float32),
        in_specs=[
            pl.BlockSpec(memory_space=pltpu.SMEM),
            pl.BlockSpec(memory_space=pltpu.VMEM),
        ],
        out_specs=pl.BlockSpec(memory_space=pltpu.VMEM),
        scratch_shapes=[
            pltpu.VMEM((quarters, 2, points // 128, 128), jnp.float32),
            pltpu.VMEM((2, points // 128, 128), jnp.float32),
            pltpu.VMEM((points, days), bf16),
            [pltpu.VMEM((groups, piece, days // FIRST_PARTS), bf16) for _ in range(FIRST_PARTS)],
            pltpu.VMEM((CHUNKS, flat, YL, piece, span), bf16),
            pltpu.VMEM((CHUNKS, YL, flat, piece, span), bf16),
            pltpu.VMEM((quarters, rows, days), bf16),
            pltpu.VMEM((CHUNKS, YL * quarters, flat, piece, span), bf16),
            dma,
            dma((quarters - 1,)),
            dma,
            dma,
            dma,
            dma((FIRST_PARTS,)),
            dma,
            dma((CHUNKS,)),
            dma,
            dma((CHUNKS, 3)),
            dma,
            dma((CHUNKS,)),
        ],
        compiler_params=pltpu.CompilerParams(
            collective_id=0, has_side_effects=True, vmem_limit_bytes=58 * 2**20
        ),
        cost_estimate=pl.CostEstimate(
            flops=2 * rows * points * days * quarters, bytes_accessed=12 * 2**20, transcendentals=0
        ),
    )(partner, series)
    correlation = total * (1.0 / (days * quarters))
    degree = jnp.sum(correlation * correlation, axis=1)
    return (correlation, degree)


def solution(mesh):
    sizes = (8, 2, 4, 2, 2)
    fine = Mesh(mesh.devices.reshape(sizes), PTS + DAYS)
    in_specs = (P(PTS, DAYS), P())
    out_specs = (P(PTS + DAYS, None), P(PTS + DAYS))
    return jax.shard_map(
        functools.partial(on_device, sizes), mesh=fine, in_specs=in_specs, out_specs=out_specs, check_vma=False
    )
```

```python
import functools

import jax
import jax.numpy as jnp
from jax import lax
from jax.experimental import pallas as pl
from jax.experimental.pallas import tpu as pltpu
from jax.sharding import Mesh, PartitionSpec as P

epsilon = 1e-06

PTS = ("z", "yl", "x")
DAYS = ("yh", "core")
FIRST_PARTS = 4
CHUNKS = 8
AHEAD = 3
LAG = 2
MESH = pl.DeviceIdType.MESH


def remote(src, dst, send, recv, **device):
    return pltpu.make_async_remote_copy(
        src_ref=src, dst_ref=dst, send_sem=send, recv_sem=recv, device_id=device, device_id_type=MESH
    )


def wait_bytes(ref, sem):
    pltpu.make_async_copy(ref, ref, sem).wait()


def kernel(
    sizes,
    partner,
    series,
    out,
    local,
    stats,
    final,
    scales,
    shift,
    factor,
    inboxes,
    chosen,
    landed,
    own,
    full,
    gate,
    local_sem,
    stat_send,
    stat_recv,
    scale_send,
    scale_recv,
    own_send,
    own_recv,
    first_send,
    first_recv,
    second_send,
    second_recv,
    y_send,
    y_recv,
    core_send,
    core_recv,
):
    Z, YL, X, YH, C = sizes
    z, yl, x, yh, core = (lax.axis_index(name) for name in PTS + DAYS)
    groups = Z * YL * X
    flat = Z * X
    quarters = YH * C
    points, days = series.shape
    piece = points // groups
    rows = points // quarters
    width = days // FIRST_PARTS
    span = days // CHUNKS
    block = (z * YL + yl) * X + x
    zx = z * X + x
    mine = yl * flat + zx
    day = yh * C + core
    here = yl * quarters + day
    tile = 128
    per_tile = tile // piece

    def peer(o):
        return (
            lax.rem(z + lax.rem(o * 3, Z), Z),
            lax.rem(yl + lax.rem(o // Z, YL), YL),
            lax.rem(x + o // (Z * YL), X),
        )

    def other_day(o):
        to = lax.rem(day + o, quarters)
        return to, lax.div(to, C), lax.rem(to, C)

    barrier = pltpu.get_barrier_semaphore()
    plane = YL * X

    def plane_peer(o):
        return {"yl": lax.rem(yl + o // X, YL), "x": lax.rem(x + o % X, X)}

    for o in range(1, plane):
        pl.semaphore_signal(barrier, inc=1, device_id=plane_peer(o), device_id_type=MESH)
    for o in range(1, Z):
        pl.semaphore_signal(barrier, inc=1, device_id={"z": lax.rem(z + o, Z)}, device_id_type=MESH)
    for o in range(1, quarters):
        _, ph, pc = other_day(o)
        pl.semaphore_signal(barrier, inc=1, device_id={"yh": ph, "core": pc}, device_id_type=MESH)
    pl.semaphore_signal(barrier, inc=1, device_id={"yl": 1 - yl, "yh": 1 - yh}, device_id_type=MESH)
    local_copy = pltpu.make_async_copy(series, local, local_sem)
    local_copy.start()
    pl.semaphore_wait(barrier, plane - 1 + Z - 1 + quarters - 1 + 1)
    for o in range(1, plane):
        pl.semaphore_signal(gate, inc=1, device_id=plane_peer(o), device_id_type=MESH)
    pl.semaphore_wait(gate, plane - 1)

    def first_part(part):
        cols = pl.ds(part * width, width)

        def send(o, carry):
            pz, py, px = peer(o)
            to = py * flat + pz * X + px
            remote(
                series.at[pl.ds(pl.multiple_of(to * piece, piece), piece), cols],
                inboxes[part].at[block],
                first_send,
                first_recv.at[part],
                z=pz,
                yl=py,
                x=px,
            ).start()
            return carry

        lax.fori_loop(1, groups, send, 0)

    first_part(0)
    local_copy.wait()

    eye = lax.broadcasted_iota(jnp.int32, (tile, tile), 0) == lax.broadcasted_iota(jnp.int32, (tile, tile), 1)

    def to_lanes(column):
        return jnp.sum(jnp.where(eye, column, 0.0), axis=0, keepdims=True)

    def to_rows(line):
        return jnp.sum(jnp.where(eye, line, 0.0), axis=1, keepdims=True)

    def local_stats(g, carry):
        values = local[pl.ds(pl.multiple_of(g * tile, tile), tile), :].astype(jnp.float32)
        mean = jnp.sum(values, axis=1, keepdims=True) / days
        centred = values - mean
        squares = jnp.sum(centred * centred, axis=1, keepdims=True)
        stats[day, g, pl.ds(0, 1), :] = to_lanes(mean)
        stats[day, g, pl.ds(1, 1), :] = to_lanes(squares)
        return carry

    lax.fori_loop(0, points // tile, local_stats, 0)
    for o in range(1, quarters):
        _, ph, pc = other_day(o)
        remote(stats.at[day], stats.at[day], stat_send, stat_recv.at[o - 1], yh=ph, core=pc).start()
    if FIRST_PARTS > 1:
        first_part(1)
    for o in range(1, quarters):
        wait_bytes(stats.at[0], stat_recv.at[o - 1])

    def whole_stats(g, carry):
        means = [stats[d, g, pl.ds(0, 1), :] for d in range(quarters)]
        average = sum(means) / quarters
        spread = sum(stats[d, g, pl.ds(1, 1), :] for d in range(quarters))
        spread += days * sum((m - average) * (m - average) for m in means)
        final[g, pl.ds(0, 1), :] = average
        final[g, pl.ds(1, 1), :] = lax.rsqrt(spread / (days * quarters) + epsilon)
        return carry

    lax.fori_loop(0, points // tile, whole_stats, 0)

    def send_scale(o, carry):
        pz, py, px = peer(o)
        to = py * flat + pz * X + px
        remote(
            final.at[to // per_tile], scales.at[block], scale_send, scale_recv, z=pz, yl=py, x=px
        ).start()
        return carry

    lax.fori_loop(1, groups, send_scale, 0)
    for o in range(1, quarters):
        to, ph, pc = other_day(o)
        remote(
            series.at[pl.ds(pl.multiple_of(to * rows, rows), rows), :],
            own.at[day],
            own_send,
            own_recv,
            yh=ph,
            core=pc,
        ).start()
    for part in range(2, FIRST_PARTS):
        first_part(part)
    for part in range(FIRST_PARTS):
        cols = pl.ds(part * width, width)
        inboxes[part][block] = local[pl.ds(pl.multiple_of(mine * piece, piece), piece), cols]
    own[day] = local[pl.ds(pl.multiple_of(day * rows, rows), rows), :]
    scales[block] = final[mine // per_tile]

    wait_bytes(scales.at[pl.ds(0, groups - 1)], scale_recv)
    lane = lax.broadcasted_iota(jnp.int32, (piece, tile), 1)
    line = lax.broadcasted_iota(jnp.int32, (piece, tile), 0) + lax.rem(mine, per_tile) * piece
    at_lane = lane == line

    def expand(b, carry):
        for which, to in ((0, shift), (1, factor)):
            column = jnp.sum(jnp.where(at_lane, scales[b, pl.ds(which, 1), :], 0.0), axis=1, keepdims=True)
            to[b] = jnp.broadcast_to(column, (piece, tile))
        return carry

    lax.fori_loop(0, groups, expand, 0)

    def normalise_own():
        def one(g, carry):
            at = pl.ds(pl.multiple_of(g * tile, tile), tile)
            average = to_rows(final[day * (rows // tile) + g, pl.ds(0, 1), :])
            scale = to_rows(final[day * (rows // tile) + g, pl.ds(1, 1), :])
            for q in range(quarters):
                values = own[q, at, :].astype(jnp.float32)
                own[q, at, :] = ((values - average) * scale).astype(jnp.bfloat16)
            return carry

        lax.fori_loop(0, rows // tile, one, 0)

    def half_of(unit):
        return 1 - yl if unit % 2 else yl

    def second_hop(unit):
        k, half = unit // 2, half_of(unit)
        inbox = inboxes[k * span // width]

        def pick(t, carry):
            source = partner[(t // X * YL + half) * X + lax.rem(t, X)]
            for j in range(0, span, tile):
                values = inbox[source, :, pl.ds(k * span % width + j, tile)].astype(jnp.float32)
                values = (values - shift[source]) * factor[source]
                chosen[k, half, t, :, pl.ds(j, tile)] = values.astype(jnp.bfloat16)
            return carry

        lax.fori_loop(0, flat, pick, 0)
        landed[k, half, zx] = chosen[k, half, zx]

        def send(o, carry):
            pz = lax.rem(z + lax.rem(o * 3, Z), Z)
            px = lax.rem(x + o // Z, X)
            remote(
                chosen.at[k, half, pz * X + px],
                landed.at[k, half, zx],
                second_send,
                second_recv.at[unit],
                z=pz,
                x=px,
            ).start()
            return carry

        lax.fori_loop(1, flat, send, 0)

    def spread_y(unit):
        k, half = unit // 2, half_of(unit)
        wait_bytes(chosen.at[k, 0, pl.ds(0, flat - 1)], second_recv.at[unit])
        if unit % 2 == 0:
            remote(landed.at[k, half], full.at[k, here], y_send, y_recv.at[k, 0], yh=1 - yh).start()
            remote(landed.at[k, half], full.at[k, here], core_send, core_recv.at[k], core=1 - core).start()
            full[k, here] = landed[k, half]
        else:
            for to in range(YH):
                remote(
                    landed.at[k, half], full.at[k, here], y_send, y_recv.at[k, 1 + yh], yl=1 - yl, yh=to
                ).start()

    def spread_core(unit):
        k = unit // 2
        if unit % 2 == 0:
            arrivals = [(0, yl * quarters + (1 - yh) * C + core)]
        else:
            arrivals = [(1 + h, (1 - yl) * quarters + h * C + core) for h in range(YH)]
        for j, at in arrivals:
            wait_bytes(full.at[k, 0], y_recv.at[k, j])
            remote(full.at[k, at], full.at[k, at], core_send, core_recv.at[k], core=1 - core).start()

    columns = min(256, flat * piece)
    tiles = flat * piece // columns

    def multiply(k, cores):
        quarter = [h * C + c for c in cores for h in range(YH)]
        group = columns // piece

        def one(n, carry):
            half, t = n // tiles, lax.rem(n, tiles)
            left = jnp.concatenate([own[q, :, pl.ds(k * span, span)] for q in quarter], axis=1)
            right = jnp.concatenate(
                [
                    full[k, half * quarters + q, pl.ds(t * group, group)].reshape(columns, span)
                    for q in quarter
                ],
                axis=1,
            )
            total = lax.dot_general(left, right, (((1,), (1,)), ((), ())), preferred_element_type=jnp.float32)
            at = pl.ds(pl.multiple_of(n * columns, columns), columns)
            out[:, at] = total if k == 0 else out[:, at] + total
            return carry

        lax.fori_loop(0, YL * tiles, one, 0)

    units = 2 * CHUNKS
    for step in range(units + AHEAD + LAG + 1):
        if step < units:
            if step // 2 * span % width == 0 and step % 2 == 0:
                part = step // 2 * span // width
                wait_bytes(inboxes[part].at[pl.ds(0, groups - 1)], first_recv.at[part])
            second_hop(step)
        unit = step - AHEAD
        if 0 <= unit < units:
            spread_y(unit)
        unit = step - AHEAD - LAG
        if 0 <= unit < units:
            spread_core(unit)
        unit = step - AHEAD - LAG - 1
        if unit > 0 and unit % 2:
            k = unit // 2
            if k == 0:
                wait_bytes(own.at[pl.ds(0, quarters - 1)], own_recv)
                normalise_own()
            if k == CHUNKS - 1:
                multiply(k, [core])
            wait_bytes(full.at[k, pl.ds(0, 4)], core_recv.at[k])
            multiply(k, [1 - core] if k == CHUNKS - 1 else range(C))

    wait_bytes(stats.at[pl.ds(0, quarters - 1)], stat_send)
    wait_bytes(own.at[pl.ds(0, quarters - 1)], own_send)
    wait_bytes(series.at[pl.ds(0, (groups - 1) * piece)], first_send)
    wait_bytes(scales.at[pl.ds(0, groups - 1)], scale_send)
    wait_bytes(chosen.at[:, :, pl.ds(0, flat - 1)], second_send)
    wait_bytes(full.at[:, pl.ds(0, 3)], y_send)
    wait_bytes(full.at[:, pl.ds(0, 4)], core_send)


def on_device(sizes, series, partner):
    Z, YL, X, YH, C = sizes
    groups, flat, quarters = Z * YL * X, Z * X, YH * C
    points, days = series.shape
    piece, rows, span = points // groups, points // quarters, days // CHUNKS
    bf16 = jnp.bfloat16
    dma = pltpu.SemaphoreType.DMA
    total = pl.pallas_call(
        functools.partial(kernel, sizes),
        out_shape=jax.ShapeDtypeStruct((rows, points), jnp.float32),
        in_specs=[
            pl.BlockSpec(memory_space=pltpu.SMEM),
            pl.BlockSpec(memory_space=pl.ANY),
        ],
        out_specs=pl.BlockSpec(memory_space=pltpu.VMEM),
        scratch_shapes=[
            pltpu.VMEM((points, days), bf16),
            pltpu.VMEM((quarters, points // 128, 2, 128), jnp.float32),
            pltpu.VMEM((points // 128, 2, 128), jnp.float32),
            pltpu.VMEM((groups, 2, 128), jnp.float32),
            pltpu.VMEM((groups, piece, 128), jnp.float32),
            pltpu.VMEM((groups, piece, 128), jnp.float32),
            [pltpu.VMEM((groups, piece, days // FIRST_PARTS), bf16) for _ in range(FIRST_PARTS)],
            pltpu.VMEM((CHUNKS, YL, flat, piece, span), bf16),
            pltpu.VMEM((CHUNKS, YL, flat, piece, span), bf16),
            pltpu.VMEM((quarters, rows, days), bf16),
            pltpu.VMEM((CHUNKS, YL * quarters, flat, piece, span), bf16),
            pltpu.SemaphoreType.REGULAR,
            dma,
            dma,
            dma((quarters - 1,)),
            dma,
            dma,
            dma,
            dma,
            dma,
            dma((FIRST_PARTS,)),
            dma,
            dma((2 * CHUNKS,)),
            dma,
            dma((CHUNKS, 3)),
            dma,
            dma((CHUNKS,)),
        ],
        compiler_params=pltpu.CompilerParams(
            collective_id=0, has_side_effects=True, vmem_limit_bytes=46 * 2**20
        ),
        cost_estimate=pl.CostEstimate(
            flops=2 * rows * points * days * quarters, bytes_accessed=12 * 2**20, transcendentals=0
        ),
    )(partner, series)
    correlation = total * (1.0 / (days * quarters))
    degree = jnp.sum(correlation * correlation, axis=1)
    return (correlation, degree)


def solution(mesh):
    sizes = (8, 2, 4, 2, 2)
    fine = Mesh(mesh.devices.reshape(sizes), PTS + DAYS)
    in_specs = (P(PTS, DAYS), P())
    out_specs = (P(PTS + DAYS, None), P(PTS + DAYS))
    return jax.shard_map(
        functools.partial(on_device, sizes), mesh=fine, in_specs=in_specs, out_specs=out_specs, check_vma=False
    )
```

```python
import functools

import jax
import jax.numpy as jnp
from jax import lax
from jax.experimental import pallas as pl
from jax.experimental.pallas import tpu as pltpu
from jax.sharding import Mesh, PartitionSpec as P

epsilon = 1e-06

PTS = ("z", "yl", "x")
DAYS = ("yh", "core")
FIRST_PARTS = 4
CHUNKS = 8
SPLIT = 2
AHEAD = 4
LAG = 3
MESH = pl.DeviceIdType.MESH


def remote(src, dst, send, recv, **device):
    return pltpu.make_async_remote_copy(
        src_ref=src, dst_ref=dst, send_sem=send, recv_sem=recv, device_id=device, device_id_type=MESH
    )


def wait_bytes(ref, sem):
    pltpu.make_async_copy(ref, ref, sem).wait()


def kernel(
    sizes,
    partner,
    series,
    out,
    local,
    stats,
    final,
    scales,
    shift,
    factor,
    inboxes,
    chosen,
    landed,
    own,
    full,
    gate,
    local_sem,
    stat_send,
    stat_recv,
    scale_send,
    scale_recv,
    own_send,
    own_recv,
    first_send,
    first_recv,
    second_send,
    second_recv,
    y_send,
    y_recv,
    core_send,
    core_recv,
):
    Z, YL, X, YH, C = sizes
    z, yl, x, yh, core = (lax.axis_index(name) for name in PTS + DAYS)
    groups = Z * YL * X
    flat = Z * X
    quarters = YH * C
    points, days = series.shape
    piece = points // groups
    rows = points // quarters
    width = days // FIRST_PARTS
    span = days // CHUNKS
    block = (z * YL + yl) * X + x
    zx = z * X + x
    mine = yl * flat + zx
    day = yh * C + core
    here = yl * quarters + day
    tile = 128
    per_tile = tile // piece

    def peer(o):
        return (
            lax.rem(z + lax.rem(o * 3, Z), Z),
            lax.rem(yl + lax.rem(o // Z, YL), YL),
            lax.rem(x + o // (Z * YL), X),
        )

    def other_day(o):
        to = lax.rem(day + o, quarters)
        return to, lax.div(to, C), lax.rem(to, C)

    barrier = pltpu.get_barrier_semaphore()
    plane = YL * X

    def plane_peer(o):
        return {"yl": lax.rem(yl + o // X, YL), "x": lax.rem(x + o % X, X)}

    for o in range(1, plane):
        pl.semaphore_signal(barrier, inc=1, device_id=plane_peer(o), device_id_type=MESH)
    for o in range(1, Z):
        pl.semaphore_signal(barrier, inc=1, device_id={"z": lax.rem(z + o, Z)}, device_id_type=MESH)
    for o in range(1, quarters):
        _, ph, pc = other_day(o)
        pl.semaphore_signal(barrier, inc=1, device_id={"yh": ph, "core": pc}, device_id_type=MESH)
    pl.semaphore_signal(barrier, inc=1, device_id={"yl": 1 - yl, "yh": 1 - yh}, device_id_type=MESH)
    local_copy = pltpu.make_async_copy(series, local, local_sem)
    local_copy.start()
    pl.semaphore_wait(barrier, plane - 1 + Z - 1 + quarters - 1 + 1)
    for o in range(1, plane):
        pl.semaphore_signal(gate, inc=1, device_id=plane_peer(o), device_id_type=MESH)

    def first_part(part, low, high):
        cols = pl.ds(part * width, width)

        def send(o, carry):
            pz, py, px = peer(o)
            to = py * flat + pz * X + px
            remote(
                series.at[pl.ds(pl.multiple_of(to * piece, piece), piece), cols],
                inboxes[part].at[block],
                first_send,
                first_recv.at[part],
                z=pz,
                yl=py,
                x=px,
            ).start()
            return carry

        lax.fori_loop(low, high, send, 0)

    first_part(0, 1, Z)
    pl.semaphore_wait(gate, plane - 1)
    first_part(0, Z, groups)
    local_copy.wait()

    eye = lax.broadcasted_iota(jnp.int32, (tile, tile), 0) == lax.broadcasted_iota(jnp.int32, (tile, tile), 1)

    def to_lanes(column):
        return jnp.sum(jnp.where(eye, column, 0.0), axis=0, keepdims=True)

    def to_rows(line):
        return jnp.sum(jnp.where(eye, line, 0.0), axis=1, keepdims=True)

    def local_stats(g, carry):
        values = local[pl.ds(pl.multiple_of(g * tile, tile), tile), :].astype(jnp.float32)
        mean = jnp.sum(values, axis=1, keepdims=True) / days
        centred = values - mean
        squares = jnp.sum(centred * centred, axis=1, keepdims=True)
        stats[day, g, pl.ds(0, 1), :] = to_lanes(mean)
        stats[day, g, pl.ds(1, 1), :] = to_lanes(squares)
        return carry

    lax.fori_loop(0, points // tile, local_stats, 0)
    for o in range(1, quarters):
        _, ph, pc = other_day(o)
        remote(stats.at[day], stats.at[day], stat_send, stat_recv.at[o - 1], yh=ph, core=pc).start()
    if FIRST_PARTS > 1:
        first_part(1, 1, groups)
    for o in range(1, quarters):
        wait_bytes(stats.at[0], stat_recv.at[o - 1])

    def whole_stats(g, carry):
        means = [stats[d, g, pl.ds(0, 1), :] for d in range(quarters)]
        average = sum(means) / quarters
        spread = sum(stats[d, g, pl.ds(1, 1), :] for d in range(quarters))
        spread += days * sum((m - average) * (m - average) for m in means)
        final[g, pl.ds(0, 1), :] = average
        final[g, pl.ds(1, 1), :] = lax.rsqrt(spread / (days * quarters) + epsilon)
        return carry

    lax.fori_loop(0, points // tile, whole_stats, 0)

    def send_scale(o, carry):
        pz, py, px = peer(o)
        to = py * flat + pz * X + px
        remote(
            final.at[to // per_tile], scales.at[block], scale_send, scale_recv, z=pz, yl=py, x=px
        ).start()
        return carry

    lax.fori_loop(1, groups, send_scale, 0)
    for o in range(1, quarters):
        to, ph, pc = other_day(o)
        remote(
            series.at[pl.ds(pl.multiple_of(to * rows, rows), rows), :],
            own.at[day],
            own_send,
            own_recv,
            yh=ph,
            core=pc,
        ).start()
    for part in range(2, FIRST_PARTS):
        first_part(part, 1, groups)
    for part in range(FIRST_PARTS):
        cols = pl.ds(part * width, width)
        inboxes[part][block] = local[pl.ds(pl.multiple_of(mine * piece, piece), piece), cols]
    own[day] = local[pl.ds(pl.multiple_of(day * rows, rows), rows), :]
    scales[block] = final[mine // per_tile]

    wait_bytes(scales.at[pl.ds(0, groups - 1)], scale_recv)
    lane = lax.broadcasted_iota(jnp.int32, (piece, tile), 1)
    line = lax.broadcasted_iota(jnp.int32, (piece, tile), 0) + lax.rem(mine, per_tile) * piece
    at_lane = lane == line

    def expand(b, carry):
        for which, to in ((0, shift), (1, factor)):
            column = jnp.sum(jnp.where(at_lane, scales[b, pl.ds(which, 1), :], 0.0), axis=1, keepdims=True)
            to[b] = jnp.broadcast_to(column, (piece, tile))
        return carry

    lax.fori_loop(0, groups, expand, 0)

    def normalise_own():
        def one(g, carry):
            at = pl.ds(pl.multiple_of(g * tile, tile), tile)
            average = to_rows(final[day * (rows // tile) + g, pl.ds(0, 1), :])
            scale = to_rows(final[day * (rows // tile) + g, pl.ds(1, 1), :])
            for q in range(quarters):
                values = own[q, at, :].astype(jnp.float32)
                own[q, at, :] = ((values - average) * scale).astype(jnp.bfloat16)
            return carry

        lax.fori_loop(0, rows // tile, one, 0)

    thin = piece // SPLIT
    per_chunk = 2 * SPLIT

    def parts_of(unit):
        k, rest = unit // per_chunk, unit % per_chunk
        rel, r = rest // SPLIT, rest % SPLIT
        return k, rel, r, 1 - yl if rel else yl, pl.ds(r * thin, thin)

    def second_hop(unit):
        k, _, _, half, lines = parts_of(unit)
        inbox = inboxes[k * span // width]

        def pick(t, carry):
            source = partner[(t // X * YL + half) * X + lax.rem(t, X)]
            for j in range(0, span, tile):
                values = inbox[source, lines, pl.ds(k * span % width + j, tile)].astype(jnp.float32)
                values = (values - shift[source, lines]) * factor[source, lines]
                chosen[k, half, t, lines, pl.ds(j, tile)] = values.astype(jnp.bfloat16)
            return carry

        lax.fori_loop(0, flat, pick, 0)
        landed[k, half, zx, lines] = chosen[k, half, zx, lines]

        def send(o, carry):
            pz = lax.rem(z + lax.rem(o * 3, Z), Z)
            px = lax.rem(x + o // Z, X)
            remote(
                chosen.at[k, half, pz * X + px, lines],
                landed.at[k, half, zx, lines],
                second_send,
                second_recv.at[unit],
                z=pz,
                x=px,
            ).start()
            return carry

        lax.fori_loop(1, flat, send, 0)

    def spread_y(unit):
        k, rel, r, half, lines = parts_of(unit)
        wait_bytes(chosen.at[k, 0, pl.ds(0, flat - 1), lines], second_recv.at[unit])
        source, target = landed.at[k, half, :, lines], full.at[k, here, :, lines]
        if rel == 0:
            remote(source, target, y_send, y_recv.at[k, 0, r], yh=1 - yh).start()
            remote(source, target, core_send, core_recv.at[k, 0], core=1 - core).start()
            full[k, here, :, lines] = landed[k, half, :, lines]
        else:
            for to in range(YH):
                remote(source, target, y_send, y_recv.at[k, 1 + yh, r], yl=1 - yl, yh=to).start()

    def spread_core(unit):
        k, rel, r, _, lines = parts_of(unit)
        if rel == 0:
            arrivals = [(0, yl * quarters + (1 - yh) * C + core)]
        else:
            arrivals = [(1 + h, (1 - yl) * quarters + h * C + core) for h in range(YH)]
        for j, at in arrivals:
            wait_bytes(full.at[k, 0, :, lines], y_recv.at[k, j, r])
            remote(
                full.at[k, at, :, lines], full.at[k, at, :, lines], core_send, core_recv.at[k, rel], core=1 - core
            ).start()

    columns = min(256, flat * piece)
    tiles = flat * piece // columns

    def multiply(k, half, cores):
        quarter = [h * C + c for c in cores for h in range(YH)]
        group = columns // piece

        def one(t, carry):
            left = jnp.concatenate([own[q, :, pl.ds(k * span, span)] for q in quarter], axis=1)
            right = jnp.concatenate(
                [
                    full[k, half * quarters + q, pl.ds(t * group, group)].reshape(columns, span)
                    for q in quarter
                ],
                axis=1,
            )
            total = lax.dot_general(left, right, (((1,), (1,)), ((), ())), preferred_element_type=jnp.float32)
            at = pl.ds(pl.multiple_of((half * tiles + t) * columns, columns), columns)
            out[:, at] = total if k == 0 else out[:, at] + total
            return carry

        lax.fori_loop(0, tiles, one, 0)

    units = per_chunk * CHUNKS
    for step in range(units + AHEAD + LAG + 1):
        if step < units:
            k = step // per_chunk
            if step % per_chunk == 0 and k * span % width == 0:
                part = k * span // width
                wait_bytes(inboxes[part].at[pl.ds(0, groups - 1)], first_recv.at[part])
            second_hop(step)
        unit = step - AHEAD
        if 0 <= unit < units:
            spread_y(unit)
        unit = step - AHEAD - LAG
        if 0 <= unit < units:
            spread_core(unit)
        unit = step - AHEAD - LAG - 1
        if unit >= 0 and unit % SPLIT == SPLIT - 1:
            k, rel, _, half, _ = parts_of(unit)
            last = unit == units - 1
            if k == 0 and rel == 0:
                wait_bytes(own.at[pl.ds(0, quarters - 1)], own_recv)
                normalise_own()
            if last:
                multiply(k, half, [core])
            wait_bytes(full.at[k, pl.ds(0, 2)], core_recv.at[k, rel])
            multiply(k, half, [1 - core] if last else range(C))

    wait_bytes(stats.at[pl.ds(0, quarters - 1)], stat_send)
    wait_bytes(own.at[pl.ds(0, quarters - 1)], own_send)
    wait_bytes(series.at[pl.ds(0, (groups - 1) * piece)], first_send)
    wait_bytes(scales.at[pl.ds(0, groups - 1)], scale_send)
    wait_bytes(chosen.at[:, :, pl.ds(0, flat - 1)], second_send)
    wait_bytes(full.at[:, pl.ds(0, 3)], y_send)
    wait_bytes(full.at[:, pl.ds(0, 4)], core_send)


def on_device(sizes, series, partner):
    Z, YL, X, YH, C = sizes
    groups, flat, quarters = Z * YL * X, Z * X, YH * C
    points, days = series.shape
    piece, rows, span = points // groups, points // quarters, days // CHUNKS
    bf16 = jnp.bfloat16
    dma = pltpu.SemaphoreType.DMA
    total = pl.pallas_call(
        functools.partial(kernel, sizes),
        out_shape=jax.ShapeDtypeStruct((rows, points), jnp.float32),
        in_specs=[
            pl.BlockSpec(memory_space=pltpu.SMEM),
            pl.BlockSpec(memory_space=pl.ANY),
        ],
        out_specs=pl.BlockSpec(memory_space=pltpu.VMEM),
        scratch_shapes=[
            pltpu.VMEM((points, days), bf16),
            pltpu.VMEM((quarters, points // 128, 2, 128), jnp.float32),
            pltpu.VMEM((points // 128, 2, 128), jnp.float32),
            pltpu.VMEM((groups, 2, 128), jnp.float32),
            pltpu.VMEM((groups, piece, 128), jnp.float32),
            pltpu.VMEM((groups, piece, 128), jnp.float32),
            [pltpu.VMEM((groups, piece, days // FIRST_PARTS), bf16) for _ in range(FIRST_PARTS)],
            pltpu.VMEM((CHUNKS, YL, flat, piece, span), bf16),
            pltpu.VMEM((CHUNKS, YL, flat, piece, span), bf16),
            pltpu.VMEM((quarters, rows, days), bf16),
            pltpu.VMEM((CHUNKS, YL * quarters, flat, piece, span), bf16),
            pltpu.SemaphoreType.REGULAR,
            dma,
            dma,
            dma((quarters - 1,)),
            dma,
            dma,
            dma,
            dma,
            dma,
            dma((FIRST_PARTS,)),
            dma,
            dma((2 * SPLIT * CHUNKS,)),
            dma,
            dma((CHUNKS, 3, SPLIT)),
            dma,
            dma((CHUNKS, 2)),
        ],
        compiler_params=pltpu.CompilerParams(
            collective_id=0, has_side_effects=True, vmem_limit_bytes=46 * 2**20
        ),
        cost_estimate=pl.CostEstimate(
            flops=2 * rows * points * days * quarters, bytes_accessed=12 * 2**20, transcendentals=0
        ),
    )(partner, series)
    correlation = total * (1.0 / (days * quarters))
    degree = jnp.sum(correlation * correlation, axis=1)
    return (correlation, degree)


def solution(mesh):
    sizes = (8, 2, 4, 2, 2)
    fine = Mesh(mesh.devices.reshape(sizes), PTS + DAYS)
    in_specs = (P(PTS, DAYS), P())
    out_specs = (P(PTS + DAYS, None), P(PTS + DAYS))
    return jax.shard_map(
        functools.partial(on_device, sizes), mesh=fine, in_specs=in_specs, out_specs=out_specs, check_vma=False
    )
```

```python
import functools

import jax
import jax.numpy as jnp
from jax import lax
from jax.experimental import pallas as pl
from jax.experimental.pallas import tpu as pltpu
from jax.sharding import Mesh, PartitionSpec as P

epsilon = 1e-06

PTS = ("z", "yl", "x")
DAYS = ("yh", "core")
FIRST_PARTS = 4
CHUNKS = 8
SPLIT = 2
AHEAD = 4
LAG = 3
MESH = pl.DeviceIdType.MESH


def remote(src, dst, send, recv, **device):
    return pltpu.make_async_remote_copy(
        src_ref=src, dst_ref=dst, send_sem=send, recv_sem=recv, device_id=device, device_id_type=MESH
    )


def wait_bytes(ref, sem):
    pltpu.make_async_copy(ref, ref, sem).wait()


def kernel(
    sizes,
    partner,
    series,
    out,
    local,
    stats,
    final,
    scales,
    shift,
    factor,
    inboxes,
    chosen,
    landed,
    own,
    full,
    gate,
    local_sem,
    stat_send,
    stat_recv,
    scale_send,
    scale_recv,
    own_send,
    own_recv,
    first_send,
    first_recv,
    second_send,
    second_recv,
    y_send,
    y_recv,
    core_send,
    core_recv,
):
    Z, YL, X, YH, C = sizes
    z, yl, x, yh, core = (lax.axis_index(name) for name in PTS + DAYS)
    groups = Z * YL * X
    flat = Z * X
    quarters = YH * C
    points, days = series.shape
    piece = points // groups
    rows = points // quarters
    width = days // FIRST_PARTS
    span = days // CHUNKS
    block = (z * YL + yl) * X + x
    zx = z * X + x
    mine = yl * flat + zx
    day = yh * C + core
    here = yl * quarters + day
    tile = 128
    per_tile = tile // piece

    def peer(o):
        return (
            lax.rem(z + lax.rem(o * 3, Z), Z),
            lax.rem(yl + lax.rem(o // Z, YL), YL),
            lax.rem(x + o // (Z * YL), X),
        )

    def other_day(o):
        to = lax.rem(day + o, quarters)
        return to, lax.div(to, C), lax.rem(to, C)

    barrier = pltpu.get_barrier_semaphore()
    plane = YL * X

    def plane_peer(o):
        return {"yl": lax.rem(yl + o // X, YL), "x": lax.rem(x + o % X, X)}

    for o in range(1, plane):
        pl.semaphore_signal(barrier, inc=1, device_id=plane_peer(o), device_id_type=MESH)
    for o in range(1, Z):
        pl.semaphore_signal(barrier, inc=1, device_id={"z": lax.rem(z + o, Z)}, device_id_type=MESH)
    for o in range(1, quarters):
        _, ph, pc = other_day(o)
        pl.semaphore_signal(barrier, inc=1, device_id={"yh": ph, "core": pc}, device_id_type=MESH)
    pl.semaphore_signal(barrier, inc=1, device_id={"yl": 1 - yl, "yh": 1 - yh}, device_id_type=MESH)
    local_copy = pltpu.make_async_copy(series, local, local_sem)
    local_copy.start()
    pl.semaphore_wait(barrier, plane - 1 + Z - 1 + quarters - 1 + 1)
    for o in range(1, plane):
        pl.semaphore_signal(gate, inc=1, device_id=plane_peer(o), device_id_type=MESH)

    def first_part(part, low, high):
        cols = pl.ds(part * width, width)

        def send(o, carry):
            pz, py, px = peer(o)
            to = py * flat + pz * X + px
            remote(
                series.at[pl.ds(pl.multiple_of(to * piece, piece), piece), cols],
                inboxes[part].at[block],
                first_send,
                first_recv.at[part],
                z=pz,
                yl=py,
                x=px,
            ).start()
            return carry

        lax.fori_loop(low, high, send, 0)

    first_part(0, 1, Z)
    pl.semaphore_wait(gate, plane - 1)
    first_part(0, Z, groups)
    for o in range(1, quarters):
        to, ph, pc = other_day(o)
        remote(
            series.at[pl.ds(pl.multiple_of(to * rows, rows), rows), :],
            own.at[day],
            own_send,
            own_recv,
            yh=ph,
            core=pc,
        ).start()
    local_copy.wait()

    eye = lax.broadcasted_iota(jnp.int32, (tile, tile), 0) == lax.broadcasted_iota(jnp.int32, (tile, tile), 1)

    def to_lanes(column):
        return jnp.sum(jnp.where(eye, column, 0.0), axis=0, keepdims=True)

    def to_rows(line):
        return jnp.sum(jnp.where(eye, line, 0.0), axis=1, keepdims=True)

    def local_stats(g, carry):
        values = local[pl.ds(pl.multiple_of(g * tile, tile), tile), :].astype(jnp.float32)
        mean = jnp.sum(values, axis=1, keepdims=True) / days
        centred = values - mean
        squares = jnp.sum(centred * centred, axis=1, keepdims=True)
        stats[day, g, pl.ds(0, 1), :] = to_lanes(mean)
        stats[day, g, pl.ds(1, 1), :] = to_lanes(squares)
        return carry

    lax.fori_loop(0, points // tile, local_stats, 0)
    for o in range(1, quarters):
        _, ph, pc = other_day(o)
        remote(stats.at[day], stats.at[day], stat_send, stat_recv.at[o - 1], yh=ph, core=pc).start()
    if FIRST_PARTS > 1:
        first_part(1, 1, groups)
    for o in range(1, quarters):
        wait_bytes(stats.at[0], stat_recv.at[o - 1])

    def whole_stats(g, carry):
        means = [stats[d, g, pl.ds(0, 1), :] for d in range(quarters)]
        average = sum(means) / quarters
        spread = sum(stats[d, g, pl.ds(1, 1), :] for d in range(quarters))
        spread += days * sum((m - average) * (m - average) for m in means)
        final[g, pl.ds(0, 1), :] = average
        final[g, pl.ds(1, 1), :] = lax.rsqrt(spread / (days * quarters) + epsilon)
        return carry

    lax.fori_loop(0, points // tile, whole_stats, 0)

    def send_scale(o, carry):
        pz, py, px = peer(o)
        to = py * flat + pz * X + px
        remote(
            final.at[to // per_tile], scales.at[block], scale_send, scale_recv, z=pz, yl=py, x=px
        ).start()
        return carry

    lax.fori_loop(1, groups, send_scale, 0)
    for part in range(2, FIRST_PARTS):
        first_part(part, 1, groups)
    for part in range(FIRST_PARTS):
        cols = pl.ds(part * width, width)
        inboxes[part][block] = local[pl.ds(pl.multiple_of(mine * piece, piece), piece), cols]
    own[day] = local[pl.ds(pl.multiple_of(day * rows, rows), rows), :]
    scales[block] = final[mine // per_tile]

    wait_bytes(scales.at[pl.ds(0, groups - 1)], scale_recv)
    lane = lax.broadcasted_iota(jnp.int32, (piece, tile), 1)
    line = lax.broadcasted_iota(jnp.int32, (piece, tile), 0) + lax.rem(mine, per_tile) * piece
    at_lane = lane == line

    def expand(b, carry):
        for which, to in ((0, shift), (1, factor)):
            column = jnp.sum(jnp.where(at_lane, scales[b, pl.ds(which, 1), :], 0.0), axis=1, keepdims=True)
            to[b] = jnp.broadcast_to(column, (piece, tile))
        return carry

    lax.fori_loop(0, groups, expand, 0)

    def normalise_own():
        def one(g, carry):
            at = pl.ds(pl.multiple_of(g * tile, tile), tile)
            average = to_rows(final[day * (rows // tile) + g, pl.ds(0, 1), :])
            scale = to_rows(final[day * (rows // tile) + g, pl.ds(1, 1), :])
            for q in range(quarters):
                values = own[q, at, :].astype(jnp.float32)
                own[q, at, :] = ((values - average) * scale).astype(jnp.bfloat16)
            return carry

        lax.fori_loop(0, rows // tile, one, 0)

    thin = piece // SPLIT
    per_chunk = 2 * SPLIT

    def parts_of(unit):
        k, rest = unit // per_chunk, unit % per_chunk
        rel, r = rest // SPLIT, rest % SPLIT
        return k, rel, r, 1 - yl if rel else yl, pl.ds(r * thin, thin)

    def second_hop(unit):
        k, _, _, half, lines = parts_of(unit)
        inbox = inboxes[k * span // width]

        def pick(t, carry):
            source = partner[(t // X * YL + half) * X + lax.rem(t, X)]
            for j in range(0, span, tile):
                values = inbox[source, lines, pl.ds(k * span % width + j, tile)].astype(jnp.float32)
                values = (values - shift[source, lines]) * factor[source, lines]
                chosen[k, half, t, lines, pl.ds(j, tile)] = values.astype(jnp.bfloat16)
            return carry

        lax.fori_loop(0, flat, pick, 0)
        landed[k, half, zx, lines] = chosen[k, half, zx, lines]

        def send(o, carry):
            pz = lax.rem(z + lax.rem(o * 3, Z), Z)
            px = lax.rem(x + o // Z, X)
            remote(
                chosen.at[k, half, pz * X + px, lines],
                landed.at[k, half, zx, lines],
                second_send,
                second_recv.at[unit],
                z=pz,
                x=px,
            ).start()
            return carry

        lax.fori_loop(1, flat, send, 0)

    def spread_y(unit):
        k, rel, r, half, lines = parts_of(unit)
        wait_bytes(chosen.at[k, 0, pl.ds(0, flat - 1), lines], second_recv.at[unit])
        source, target = landed.at[k, half, :, lines], full.at[k, here, :, lines]
        if rel == 0:
            remote(source, target, y_send, y_recv.at[k, 0, r], yh=1 - yh).start()
            remote(source, target, core_send, core_recv.at[k, 0], core=1 - core).start()
            full[k, here, :, lines] = landed[k, half, :, lines]
        else:
            for to in range(YH):
                remote(source, target, y_send, y_recv.at[k, 1 + yh, r], yl=1 - yl, yh=to).start()

    def spread_core(unit):
        k, rel, r, _, lines = parts_of(unit)
        if rel == 0:
            arrivals = [(0, yl * quarters + (1 - yh) * C + core)]
        else:
            arrivals = [(1 + h, (1 - yl) * quarters + h * C + core) for h in range(YH)]
        for j, at in arrivals:
            wait_bytes(full.at[k, 0, :, lines], y_recv.at[k, j, r])
            remote(
                full.at[k, at, :, lines], full.at[k, at, :, lines], core_send, core_recv.at[k, rel], core=1 - core
            ).start()

    columns = min(256, flat * piece)
    tiles = flat * piece // columns

    def multiply(k, half, cores):
        quarter = [h * C + c for c in cores for h in range(YH)]
        group = columns // piece

        def one(t, carry):
            left = jnp.concatenate([own[q, :, pl.ds(k * span, span)] for q in quarter], axis=1)
            right = jnp.concatenate(
                [
                    full[k, half * quarters + q, pl.ds(t * group, group)].reshape(columns, span)
                    for q in quarter
                ],
                axis=1,
            )
            total = lax.dot_general(left, right, (((1,), (1,)), ((), ())), preferred_element_type=jnp.float32)
            at = pl.ds(pl.multiple_of((half * tiles + t) * columns, columns), columns)
            out[:, at] = total if k == 0 else out[:, at] + total
            return carry

        lax.fori_loop(0, tiles, one, 0)

    units = per_chunk * CHUNKS
    for step in range(units + AHEAD + LAG + 1):
        if step < units:
            k = step // per_chunk
            if step % per_chunk == 0 and k * span % width == 0:
                part = k * span // width
                wait_bytes(inboxes[part].at[pl.ds(0, groups - 1)], first_recv.at[part])
            second_hop(step)
        unit = step - AHEAD
        if 0 <= unit < units:
            spread_y(unit)
        unit = step - AHEAD - LAG
        if 0 <= unit < units:
            spread_core(unit)
        unit = step - AHEAD - LAG - 1
        if unit >= 0 and unit % SPLIT == SPLIT - 1:
            k, rel, _, half, _ = parts_of(unit)
            last = unit == units - 1
            if k == 0 and rel == 0:
                wait_bytes(own.at[pl.ds(0, quarters - 1)], own_recv)
                normalise_own()
            if last:
                multiply(k, half, [core])
            wait_bytes(full.at[k, pl.ds(0, 2)], core_recv.at[k, rel])
            multiply(k, half, [1 - core] if last else range(C))

    wait_bytes(stats.at[pl.ds(0, quarters - 1)], stat_send)
    wait_bytes(own.at[pl.ds(0, quarters - 1)], own_send)
    wait_bytes(series.at[pl.ds(0, (groups - 1) * piece)], first_send)
    wait_bytes(scales.at[pl.ds(0, groups - 1)], scale_send)
    wait_bytes(chosen.at[:, :, pl.ds(0, flat - 1)], second_send)
    wait_bytes(full.at[:, pl.ds(0, 3)], y_send)
    wait_bytes(full.at[:, pl.ds(0, 4)], core_send)


def on_device(sizes, series, partner):
    Z, YL, X, YH, C = sizes
    groups, flat, quarters = Z * YL * X, Z * X, YH * C
    points, days = series.shape
    piece, rows, span = points // groups, points // quarters, days // CHUNKS
    bf16 = jnp.bfloat16
    dma = pltpu.SemaphoreType.DMA
    total = pl.pallas_call(
        functools.partial(kernel, sizes),
        out_shape=jax.ShapeDtypeStruct((rows, points), jnp.float32),
        in_specs=[
            pl.BlockSpec(memory_space=pltpu.SMEM),
            pl.BlockSpec(memory_space=pl.ANY),
        ],
        out_specs=pl.BlockSpec(memory_space=pltpu.VMEM),
        scratch_shapes=[
            pltpu.VMEM((points, days), bf16),
            pltpu.VMEM((quarters, points // 128, 2, 128), jnp.float32),
            pltpu.VMEM((points // 128, 2, 128), jnp.float32),
            pltpu.VMEM((groups, 2, 128), jnp.float32),
            pltpu.VMEM((groups, piece, 128), jnp.float32),
            pltpu.VMEM((groups, piece, 128), jnp.float32),
            [pltpu.VMEM((groups, piece, days // FIRST_PARTS), bf16) for _ in range(FIRST_PARTS)],
            pltpu.VMEM((CHUNKS, YL, flat, piece, span), bf16),
            pltpu.VMEM((CHUNKS, YL, flat, piece, span), bf16),
            pltpu.VMEM((quarters, rows, days), bf16),
            pltpu.VMEM((CHUNKS, YL * quarters, flat, piece, span), bf16),
            pltpu.SemaphoreType.REGULAR,
            dma,
            dma,
            dma((quarters - 1,)),
            dma,
            dma,
            dma,
            dma,
            dma,
            dma((FIRST_PARTS,)),
            dma,
            dma((2 * SPLIT * CHUNKS,)),
            dma,
            dma((CHUNKS, 3, SPLIT)),
            dma,
            dma((CHUNKS, 2)),
        ],
        compiler_params=pltpu.CompilerParams(
            collective_id=0, has_side_effects=True, vmem_limit_bytes=46 * 2**20
        ),
        cost_estimate=pl.CostEstimate(
            flops=2 * rows * points * days * quarters, bytes_accessed=12 * 2**20, transcendentals=0
        ),
    )(partner, series)
    correlation = total * (1.0 / (days * quarters))
    degree = jnp.sum(correlation * correlation, axis=1)
    return (correlation, degree)


def solution(mesh):
    sizes = (8, 2, 4, 2, 2)
    fine = Mesh(mesh.devices.reshape(sizes), PTS + DAYS)
    in_specs = (P(PTS, DAYS), P())
    out_specs = (P(PTS + DAYS, None), P(PTS + DAYS))
    return jax.shard_map(
        functools.partial(on_device, sizes), mesh=fine, in_specs=in_specs, out_specs=out_specs, check_vma=False
    )
```
